128 devices in a mesh: feat: 8 (over x, core), rows: 16 (over z, y).
Axes of the slice: x: 4, y: 4, z: 4, core: 2. Of those that a mesh axis runs over, the one named last changes fastest.
Arguments:
- features: bfloat16 [128, 128, 768], P('feat', None, 'rows'), may hold values from -6 to 6
- w_in: bfloat16 [128, 256], replicated, may hold values from -0.5 to 0.5
- bias: float32 [256], replicated, may hold values from -4 to 4
- tiles: bfloat16 [768, 8, 128, 128], P(('feat', 'rows')), may hold values from 0 to 1, as said below
- tile_cols: int32 [768, 8], P(('feat', 'rows')), may hold values from 0 to 767, as said below
- tile_counts: int32 [768], P(('feat', 'rows')), may hold values from 1 to 8, as said below
- cotangent: bfloat16 [98304, 256], P(('feat', 'rows')), may hold values from -6 to 6
Outputs:
- hidden: bfloat16 [98304, 256], P(('feat', 'rows'))
- weight_grad: float32 [128, 256], P('feat')
The draws below stay inside these ranges and needn't reach their ends.
Inputs may be any that keep to these rules, and one draw needn't show every extreme that they name: Each block row's count lies between 1 and 8; in every draw some device owns a block row with 8 live slots. Slots k >= tile_counts[I] are ignored. `tile_cols`: block row I on the device owning blocks s * 6 to s * 6 + 6 - 1 (s = I // 6) names column blocks J with J // 96 = I // 96 and (J - (s % 16) * 6 + 2) mod 96 below 10: its own blocks or up to 2 blocks of the neighbouring devices in its cycle, wrapping; both ends are reached. `tiles`: entries are 0 or 1.
All inputs are finite; a program needn't handle non-finite values.
Results may differ from the reference program's by a relative error of at most 0.008.
Values may be sent and summed in bfloat16 or wider, within the bound.
No kernel may reach another device: no remote copies, remote signals or barrier semaphores. Data moves between devices by JAX's collectives and lax.ppermute only.
A program may use at most 64 MiB of HBM per device.

```python
import jax
import jax.numpy as jnp
from jax import lax

F = 128
H = 256
B = 128
K = 8
NB = 6
HALO_BLK = 2
ROWS_DEV = 768
NODES = 98304
NBLK = 768
CYCLE = 96
N_FEAT = 8
DEVICES = 128


def draw_tiles(key, part):
    values = jax.random.randint(key, (NBLK, K, B, B), 0, 8)
    return (values == 0).astype(jnp.float32).astype(jnp.bfloat16)


def draw_tile_cols(key, part):
    blocks = jnp.arange(NBLK, dtype=jnp.int32)
    group = blocks // CYCLE
    shard = blocks % CYCLE // NB
    offset = jax.random.randint(key, (NBLK, K), 0, NB + 2 * HALO_BLK)
    position = (shard[:, None] * NB - HALO_BLK + offset) % CYCLE
    return (group[:, None] * CYCLE + position).astype(jnp.int32)


def draw_tile_counts(key, part):
    first, second, third, fourth = jax.random.split(key, 4)
    owners = jnp.arange(DEVICES, dtype=jnp.int32)
    limits = jax.random.randint(first, (DEVICES,), 2, K + 1)
    chosen = jax.random.randint(second, (), 0, DEVICES)
    limits = jnp.where(owners == chosen, K, limits)
    lowest = (limits + 1) // 2
    counts = jax.random.randint(third, (DEVICES, NB), lowest[:, None], limits[:, None] + 1)
    marked = jax.random.randint(fourth, (DEVICES,), 0, NB)
    counts = jnp.where(jnp.arange(NB, dtype=jnp.int32)[None, :] == marked[:, None], limits[:, None], counts)
    return counts.reshape(NBLK).astype(jnp.int32)


def shard_levels(key, dims, cuts, smallest, high):
    gain = 1.0
    for axis_at, blocks in cuts:
        heights = jax.random.uniform(jax.random.fold_in(jax.random.fold_in(key, 6), axis_at), (blocks,), jnp.float32, smallest / len(cuts), high / len(cuts))
        gain = gain * jnp.repeat(jnp.exp(heights), dims[axis_at] // blocks).reshape((-1,) + (1,) * (len(dims) - 1 - axis_at))
    return gain


def scatter_about(key, dims, spread, bound, cuts=(), kind=jnp.bfloat16):
    entries = spread * jax.random.normal(key, dims, jnp.float32)
    if cuts:
        entries = entries * shard_levels(key, dims, cuts, -0.22, 0.18)
    return jnp.clip(entries, -bound, bound).astype(kind)


def setup_inputs(seed: int = 0) -> dict:
    keys = jax.random.split(jax.random.key(seed), 8)
    return {
        "features": scatter_about(keys[0], (F, DEVICES, ROWS_DEV), 1.0, 6.0, ((0, 8), (2, 16))),
        "w_in": scatter_about(keys[1], (F, H), F ** -0.5, 0.5),
        "bias": scatter_about(keys[2], (H,), 1.0, 4.0, (), jnp.float32),
        "tiles": draw_tiles(jax.random.fold_in(keys[7], 71), 0),
        "tile_cols": draw_tile_cols(jax.random.fold_in(keys[7], 71), 0),
        "tile_counts": draw_tile_counts(jax.random.fold_in(keys[7], 71), 0),
        "cotangent": scatter_about(keys[6], (NODES, H), 1.0, 6.0, ((0, 128),)),
    }


def gelu_parts(values):
    inner = 0.7978845608 * (values + 0.044715 * values * values * values)
    tangent = jnp.tanh(inner)
    output = 0.5 * values * (1.0 + tangent)
    slope = 0.5 * (1.0 + tangent) + 0.5 * values * (1.0 - tangent * tangent) * 0.7978845608 * (1.0 + 3.0 * 0.044715 * values * values)
    return output, slope


def reference(features, w_in, bias, tiles, tile_cols, tile_counts, cotangent):
    slice_width = F // N_FEAT
    flat = features.reshape(F, NODES)
    summed = jnp.zeros((NODES, H), jnp.float32)
    for group in range(N_FEAT):
        partial_value = jnp.dot(flat[group * slice_width:(group + 1) * slice_width].T, w_in[group * slice_width:(group + 1) * slice_width], preferred_element_type=jnp.float32)
        partial_value = lax.optimization_barrier(partial_value.astype(jnp.bfloat16))
        summed = summed + partial_value.astype(jnp.float32)
    projected = summed.astype(jnp.bfloat16).reshape(NBLK, B, H)
    slot_ids = jnp.arange(K, dtype=jnp.int32)
    tile_groups = tiles.reshape(DEVICES, NB, K, B, B)
    col_groups = tile_cols.reshape(DEVICES, NB, K)
    count_groups = tile_counts.reshape(DEVICES, NB)

    def masked_tiles(tile_block, count_block):
        live_slot = (slot_ids[None, :] < count_block[:, None]).astype(jnp.bfloat16)
        return (tile_block * live_slot[:, :, None, None]).astype(jnp.float32)

    def forward(inputs):
        tile_block, col_block, count_block, own_block = inputs
        masked = masked_tiles(tile_block, count_block)
        degree = jnp.sum(masked, axis=(1, 3))
        neighbours = projected[col_block].astype(jnp.float32)
        summed_rows = jnp.einsum('bkij,bkjh->bih', masked, neighbours)
        pre_act = (own_block.astype(jnp.float32) + summed_rows) / (degree[:, :, None] + 1.0) + bias
        return pre_act, degree

    pre_act, degree = lax.map(forward, (tile_groups, col_groups, count_groups, projected.reshape(DEVICES, NB, B, H)))
    activated, slope = gelu_parts(pre_act)
    hidden = activated.astype(jnp.bfloat16).reshape(NODES, H)
    scaled = (cotangent.reshape(DEVICES, NB, B, H).astype(jnp.float32) * slope / (degree[:, :, :, None] + 1.0)).astype(jnp.bfloat16)

    def backward(carry, inputs):
        tile_block, col_block, count_block, scaled_block = inputs
        masked = masked_tiles(tile_block, count_block)
        terms = jnp.einsum('bkij,bih->bkjh', masked, scaled_block.astype(jnp.float32))
        return carry.at[col_block.reshape(-1)].add(terms.reshape(NB * K, B, H)), None

    total, unused = lax.scan(backward, scaled.reshape(NBLK, B, H).astype(jnp.float32), (tile_groups, col_groups, count_groups, scaled))
    grad_proj = total.astype(jnp.bfloat16).reshape(NODES, H)
    weight_grad = jnp.dot(flat, grad_proj, preferred_element_type=jnp.float32)
    return hidden, weight_grad
```

```python
import jax
import jax.numpy as jnp
from jax import lax
from jax.experimental import pallas as pl
from jax.experimental.pallas import tpu as pltpu
from jax.sharding import PartitionSpec as P

HALO_BLK = 2
F32 = jnp.float32
BF16 = jnp.bfloat16


def adjacency_kernel(cols_ref, counts_ref, base_ref, tiles_ref, adj_ref, *, rows_axis, cycle):
    nb, slots, side, _ = tiles_ref.shape
    adj_ref[...] = jnp.zeros_like(adj_ref)
    eye = (
        lax.broadcasted_iota(jnp.int32, (side, side), 0)
        == lax.broadcasted_iota(jnp.int32, (side, side), 1)
    )
    eye = jnp.where(eye, 1.0, 0.0).astype(BF16)
    base = base_ref[0]
    for b in range(nb):
        rows = pl.ds(b * side, side)
        adj_ref[rows, pl.ds((b + HALO_BLK) * side, side)] = eye
        for k in range(slots):

            @pl.when(k < counts_ref[b])
            def _():
                block = lax.rem(cols_ref[b, k] - base + HALO_BLK + cycle, cycle)
                at = (rows, pl.ds(pl.multiple_of(block * side, side), side))
                adj_ref[at] = adj_ref[at] + tiles_ref[b, k]


def layer_kernel(recv_ref, adj_ref, w_ref, bias_ref, cot_ref, hidden_ref, grad_ref, x_ref):
    groups, senders, width, lanes = recv_ref.shape
    features = groups * width
    nodes = hidden_ref.shape[0]
    ext = x_ref.shape[0]
    halo = (ext - nodes) // 2
    part = nodes // senders
    x_ref[:, features:] = jnp.ones((ext, features), BF16)
    for r in range(senders):
        piece = recv_ref[:, r].reshape(features, lanes)
        piece = jnp.concatenate([piece, jnp.zeros((features, 128 - lanes), BF16)], axis=1).T
        x_ref[halo + r * part : halo + (r + 1) * part, :features] = piece[:part]
        first, last = r * part, (r + 1) * part
        if first < halo:
            n = min(last, halo) - first
            x_ref[halo + nodes + first : halo + nodes + first + n, :features] = piece[part : part + n]
        if last > nodes - halo:
            skip = max(nodes - halo - first, 0)
            to = first + skip - (nodes - halo)
            x_ref[to : to + part - skip, :features] = piece[part + skip : 2 * part]
    w = w_ref[...]
    ww = jnp.concatenate([w, w], axis=0)
    bias = bias_ref[...]
    side = 128
    hidden_width = w.shape[1]
    total = jnp.zeros((2 * features, hidden_width), F32)
    for b in range(nodes // side):
        rows = pl.ds(b * side, side)
        both = jnp.dot(adj_ref[rows, :], x_ref[...], preferred_element_type=F32)
        y = both[:, :features]
        inv = 1.0 / both[:, features:]
        inv = jnp.concatenate([inv] * (hidden_width // features), axis=1)
        y_hi = y.astype(BF16)
        y_lo = (y - y_hi.astype(F32)).astype(BF16)
        yy = jnp.concatenate([y_hi, y_lo], axis=1)
        v = jnp.dot(yy, ww, preferred_element_type=F32) * inv + bias
        v2 = v * v
        t = jnp.tanh(0.7978845608 * (v + 0.044715 * v2 * v))
        half = 0.5 * (1.0 + t)
        hidden_ref[rows, :] = (v * half).astype(BF16)
        slope = half + 0.5 * v * (1.0 - t * t) * 0.7978845608 * (1.0 + 3.0 * 0.044715 * v2)
        scaled = (cot_ref[rows, :].astype(F32) * slope * inv).astype(BF16)
        total += lax.dot_general(yy, scaled, (((0,), (0,)), ((), ())), preferred_element_type=F32)
    grad_ref[...] = total[:features] + total[features:]


def body(features, w_in, bias, tiles, tile_cols, tile_counts, cotangent):
    block_rows, slots, side, _ = tiles.shape
    n_features, hidden_width = w_in.shape
    feat_size = lax.axis_size("feat")
    row_size = lax.axis_size("rows")
    nodes = block_rows * side
    halo = HALO_BLK * side
    width, owners, part = features.shape
    feat_id = lax.axis_index("feat")
    row_id = lax.axis_index("rows")
    cycle = block_rows * row_size

    by_owner = features.transpose(1, 0, 2)
    ring = by_owner.reshape(feat_size, row_size, width, part)
    beside = jnp.where(row_id * 2 < row_size, jnp.roll(ring, -1, axis=1), jnp.roll(ring, 1, axis=1))
    send = jnp.concatenate([by_owner, beside.reshape(by_owner.shape)], axis=2)
    recv = lax.all_to_all(send, ("feat", "rows"), split_axis=0, concat_axis=0, tiled=True)
    recv = recv.reshape(feat_size, row_size, width, 2 * part)

    base = (feat_id * cycle + row_id * block_rows).reshape(1).astype(jnp.int32)
    ext = nodes + 2 * halo
    vmem = pl.BlockSpec(memory_space=pltpu.VMEM)
    smem = pl.BlockSpec(memory_space=pltpu.SMEM)
    adj = pl.pallas_call(
        lambda *refs: adjacency_kernel(*refs, rows_axis="rows", cycle=cycle),
        out_shape=jax.ShapeDtypeStruct((nodes, ext), BF16),
        in_specs=[smem, smem, smem, vmem],
        out_specs=vmem,
        compiler_params=pltpu.CompilerParams(vmem_limit_bytes=16 * 2**20),
        cost_estimate=pl.CostEstimate(flops=2 * 10**6, bytes_accessed=4 * 10**6, transcendentals=0),
        name="adjacency",
    )(tile_cols, tile_counts, base, tiles)
    hidden, terms = pl.pallas_call(
        layer_kernel,
        out_shape=(
            jax.ShapeDtypeStruct((nodes, hidden_width), BF16),
            jax.ShapeDtypeStruct((n_features, hidden_width), F32),
        ),
        in_specs=[vmem] * 5,
        out_specs=(vmem, vmem),
        scratch_shapes=[pltpu.VMEM((ext, 2 * n_features), BF16)],
        compiler_params=pltpu.CompilerParams(vmem_limit_bytes=24 * 2**20),
        cost_estimate=pl.CostEstimate(flops=600 * 10**6, bytes_accessed=4 * 10**6, transcendentals=nodes * hidden_width),
        name="layer",
    )(recv, adj, w_in, bias.reshape(1, hidden_width), cotangent)

    pieces = lax.all_to_all(terms.reshape(feat_size, width, hidden_width), "feat", split_axis=0, concat_axis=0, tiled=True)
    mine = jnp.sum(pieces, axis=0)
    copies = jnp.broadcast_to(mine[None], (row_size, width, hidden_width))
    pieces = lax.all_to_all(copies, "rows", split_axis=0, concat_axis=0, tiled=True)
    return hidden, jnp.sum(pieces, axis=0)


def solution(mesh):
    in_specs = (
        P("feat", None, "rows"),
        P(),
        P(),
        P(("feat", "rows"), None, None, None),
        P(("feat", "rows"), None),
        P(("feat", "rows")),
        P(("feat", "rows"), None),
    )
    out_specs = (P(("feat", "rows"), None), P("feat", None))
    return jax.shard_map(body, mesh=mesh, in_specs=in_specs, out_specs=out_specs, check_vma=False)
```

```python
import jax
import jax.numpy as jnp
from jax import lax
from jax.experimental import pallas as pl
from jax.experimental.pallas import tpu as pltpu
from jax.sharding import PartitionSpec as P

HALO_BLK = 2
LANES = 128
CHUNK = 256
GELU_A, GELU_B = 0.7978845608, 0.044715
F32 = jnp.float32
BF16 = jnp.bfloat16


def adjacency_kernel(cols_ref, counts_ref, base_ref, tiles_ref, adj_ref, *, cycle):
    nb, slots, side, _ = tiles_ref.shape
    adj_ref[...] = jnp.zeros_like(adj_ref)
    eye = (
        lax.broadcasted_iota(jnp.int32, (side, side), 0)
        == lax.broadcasted_iota(jnp.int32, (side, side), 1)
    )
    eye = jnp.where(eye, 1.0, 0.0).astype(BF16)
    base = base_ref[0]
    for b in range(nb):
        rows = pl.ds(b * side, side)
        adj_ref[rows, pl.ds((b + HALO_BLK) * side, side)] = eye
        for k in range(slots):

            @pl.when(k < counts_ref[b])
            def _():
                block = lax.rem(cols_ref[b, k] - base + HALO_BLK + cycle, cycle)
                at = (rows, pl.ds(pl.multiple_of(block * side, side), side))
                adj_ref[at] = adj_ref[at] + tiles_ref[b, k]


def send_kernel(step_ref, x_ref, out_ref, rows_ref, *, ring):
    width, part, owners = x_ref.shape
    i = lax.broadcasted_iota(jnp.int32, (owners, owners), 0)
    k = lax.broadcasted_iota(jnp.int32, (owners, owners), 1)
    beside = (i // ring) * ring + lax.rem(lax.rem(i, ring) + step_ref[0] + ring, ring)
    pick = jnp.concatenate([jnp.where(k == i, 1.0, 0.0), jnp.where(k == beside, 1.0, 0.0)], axis=1).astype(BF16)
    none = jnp.zeros((part, owners), BF16)
    rest = jnp.zeros((LANES - 2 * part, 2 * owners), BF16)
    for c in range(width):
        x = x_ref[c]
        spread = jnp.concatenate(
            [jnp.concatenate([x, none], axis=1), jnp.concatenate([none, x], axis=1), rest], axis=0
        )
        rows_ref[pl.ds(c, owners, stride=width), :] = lax.dot_general(
            pick, spread, (((1,), (1,)), ((), ())), preferred_element_type=F32
        )
    out_ref[...] = rows_ref[...].astype(BF16).reshape(out_ref.shape)


def layer_kernel(recv_ref, adj_ref, w_ref, bias_ref, cot_ref, hidden_ref, grad_ref, x_ref):
    groups, senders, width, lanes = recv_ref.shape
    features = groups * width
    nodes = hidden_ref.shape[0]
    ext = x_ref.shape[0]
    halo = (ext - nodes) // 2
    part = nodes // senders
    x_ref[:, features:] = jnp.ones((ext, features), BF16)
    for r in range(senders):
        piece = recv_ref[:, r].reshape(features, lanes).T
        x_ref[halo + r * part : halo + (r + 1) * part, :features] = piece[:part]
        first, last = r * part, (r + 1) * part
        if first < halo:
            n = min(last, halo) - first
            x_ref[halo + nodes + first : halo + nodes + first + n, :features] = piece[part : part + n]
        if last > nodes - halo:
            skip = max(nodes - halo - first, 0)
            to = first + skip - (nodes - halo)
            x_ref[to : to + part - skip, :features] = piece[part + skip : 2 * part]
    w = w_ref[...]
    ww = jnp.concatenate([w, w], axis=0)
    bias = bias_ref[...]
    hidden_width = w.shape[1]
    total = jnp.zeros((2 * features, hidden_width), F32)
    for b in range(nodes // CHUNK):
        rows = pl.ds(b * CHUNK, CHUNK)
        both = jnp.dot(adj_ref[rows, :], x_ref[...], preferred_element_type=F32)
        y = both[:, :features]
        inv = 1.0 / both[:, features:]
        inv = jnp.concatenate([inv] * (hidden_width // features), axis=1)
        y_hi = y.astype(BF16)
        y_lo = (y - y_hi.astype(F32)).astype(BF16)
        yy = jnp.concatenate([y_hi, y_lo], axis=1)
        v = jnp.dot(yy, ww, preferred_element_type=F32) * inv + bias
        v2 = v * v
        t = jnp.tanh(v * (GELU_A + (GELU_A * GELU_B) * v2))
        half = 0.5 + 0.5 * t
        h = v * half
        hidden_ref[rows, :] = h.astype(BF16)
        slope = half + h * (1.0 - t) * (GELU_A + (3.0 * GELU_A * GELU_B) * v2)
        scaled = (cot_ref[rows, :].astype(F32) * inv * slope).astype(BF16)
        total += lax.dot_general(yy, scaled, (((0,), (0,)), ((), ())), preferred_element_type=F32)
    grad_ref[...] = total[:features] + total[features:]


def body(features, w_in, bias, tiles, tile_cols, tile_counts, cotangent):
    block_rows, slots, side, _ = tiles.shape
    n_features, hidden_width = w_in.shape
    feat_size = lax.axis_size("feat")
    row_size = lax.axis_size("rows")
    nodes = block_rows * side
    halo = HALO_BLK * side
    width, owners, part = features.shape
    feat_id = lax.axis_index("feat")
    row_id = lax.axis_index("rows")
    cycle = block_rows * row_size

    vmem = pl.BlockSpec(memory_space=pltpu.VMEM)
    smem = pl.BlockSpec(memory_space=pltpu.SMEM)
    step = jnp.where(row_id * 2 < row_size, 1, -1).reshape(1).astype(jnp.int32)
    send = pl.pallas_call(
        lambda *refs: send_kernel(*refs, ring=row_size),
        out_shape=jax.ShapeDtypeStruct((owners, width, LANES), BF16),
        in_specs=[smem, vmem],
        out_specs=vmem,
        scratch_shapes=[pltpu.VMEM((owners * width, LANES), F32)],
        compiler_params=pltpu.CompilerParams(vmem_limit_bytes=8 * 2**20),
        name="pieces",
    )(step, features.transpose(0, 2, 1))
    recv = lax.all_to_all(send, ("feat", "rows"), split_axis=0, concat_axis=0, tiled=True)
    recv = recv.reshape(feat_size, row_size, width, LANES)

    base = (feat_id * cycle + row_id * block_rows).reshape(1).astype(jnp.int32)
    ext = nodes + 2 * halo
    adj = pl.pallas_call(
        lambda *refs: adjacency_kernel(*refs, cycle=cycle),
        out_shape=jax.ShapeDtypeStruct((nodes, ext), BF16),
        in_specs=[smem, smem, smem, vmem],
        out_specs=vmem,
        compiler_params=pltpu.CompilerParams(vmem_limit_bytes=16 * 2**20),
        cost_estimate=pl.CostEstimate(flops=2 * 10**6, bytes_accessed=4 * 10**6, transcendentals=0),
        name="adjacency",
    )(tile_cols, tile_counts, base, tiles)
    hidden, terms = pl.pallas_call(
        layer_kernel,
        out_shape=(
            jax.ShapeDtypeStruct((nodes, hidden_width), BF16),
            jax.ShapeDtypeStruct((n_features, hidden_width), F32),
        ),
        in_specs=[vmem] * 5,
        out_specs=(vmem, vmem),
        scratch_shapes=[pltpu.VMEM((ext, 2 * n_features), BF16)],
        compiler_params=pltpu.CompilerParams(vmem_limit_bytes=24 * 2**20),
        cost_estimate=pl.CostEstimate(flops=600 * 10**6, bytes_accessed=4 * 10**6, transcendentals=nodes * hidden_width),
        name="layer",
    )(recv, adj, w_in, bias.reshape(1, hidden_width), cotangent)

    pieces = lax.all_to_all(terms.reshape(feat_size, width, hidden_width), "feat", split_axis=0, concat_axis=0, tiled=True)
    mine = jnp.sum(pieces, axis=0)
    copies = jnp.broadcast_to(mine[None], (row_size, width, hidden_width))
    pieces = lax.all_to_all(copies, "rows", split_axis=0, concat_axis=0, tiled=True)
    return hidden, jnp.sum(pieces, axis=0)


def solution(mesh):
    in_specs = (
        P("feat", None, "rows"),
        P(),
        P(),
        P(("feat", "rows"), None, None, None),
        P(("feat", "rows"), None),
        P(("feat", "rows")),
        P(("feat", "rows"), None),
    )
    out_specs = (P(("feat", "rows"), None), P("feat", None))
    return jax.shard_map(body, mesh=mesh, in_specs=in_specs, out_specs=out_specs, check_vma=False)
```

```python
import jax
import jax.numpy as jnp
from jax import lax
from jax.experimental import pallas as pl
from jax.experimental.pallas import tpu as pltpu
from jax.sharding import PartitionSpec as P

HALO_BLK = 2
LANES = 128
CORES = 2
FEAT = ("x", "core")
ALL = ("x", "core", "rows")
CHUNK = 256
GELU_A, GELU_B = 0.7978845608, 0.044715
F32 = jnp.float32
BF16 = jnp.bfloat16


def adjacency_kernel(cols_ref, counts_ref, base_ref, tiles_ref, adj_ref, *, cycle):
    nb, slots, side, _ = tiles_ref.shape
    adj_ref[...] = jnp.zeros_like(adj_ref)
    eye = (
        lax.broadcasted_iota(jnp.int32, (side, side), 0)
        == lax.broadcasted_iota(jnp.int32, (side, side), 1)
    )
    eye = jnp.where(eye, 1.0, 0.0).astype(BF16)
    base = base_ref[0]
    for b in range(nb):
        rows = pl.ds(b * side, side)
        adj_ref[rows, pl.ds((b + HALO_BLK) * side, side)] = eye
        for k in range(slots):

            @pl.when(k < counts_ref[b])
            def _():
                block = lax.rem(cols_ref[b, k] - base + HALO_BLK + cycle, cycle)
                at = (rows, pl.ds(pl.multiple_of(block * side, side), side))
                adj_ref[at] = adj_ref[at] + tiles_ref[b, k]


def send_kernel(step_ref, x_ref, out_ref, rows_ref, *, ring):
    width, part, owners = x_ref.shape
    i = lax.broadcasted_iota(jnp.int32, (owners, owners), 0)
    k = lax.broadcasted_iota(jnp.int32, (owners, owners), 1)
    beside = (i // ring) * ring + lax.rem(lax.rem(i, ring) + step_ref[0] + ring, ring)
    pick = jnp.concatenate([jnp.where(k == i, 1.0, 0.0), jnp.where(k == beside, 1.0, 0.0)], axis=1).astype(BF16)
    none = jnp.zeros((part, owners), BF16)
    rest = jnp.zeros((LANES - 2 * part, 2 * owners), BF16)
    for c in range(width):
        x = x_ref[c]
        spread = jnp.concatenate(
            [jnp.concatenate([x, none], axis=1), jnp.concatenate([none, x], axis=1), rest], axis=0
        )
        rows_ref[pl.ds(c, owners, stride=width), :] = lax.dot_general(
            pick, spread, (((1,), (1,)), ((), ())), preferred_element_type=F32
        )
    out_ref[...] = rows_ref[...].astype(BF16).reshape(out_ref.shape)


def layer_kernel(recv_ref, adj_ref, w_ref, bias_ref, cot_ref, core_ref, hidden_ref, mine_ref, other_ref, x_ref):
    groups, senders, width, lanes = recv_ref.shape
    features = groups * width
    nodes = hidden_ref.shape[0]
    ext = x_ref.shape[0]
    halo = (ext - nodes) // 2
    part = nodes // senders
    x_ref[:, features:] = jnp.ones((ext, features), BF16)
    for r in range(senders):
        piece = recv_ref[:, r].reshape(features, lanes).T
        x_ref[halo + r * part : halo + (r + 1) * part, :features] = piece[:part]
        first, last = r * part, (r + 1) * part
        if first < halo:
            n = min(last, halo) - first
            x_ref[halo + nodes + first : halo + nodes + first + n, :features] = piece[part : part + n]
        if last > nodes - halo:
            skip = max(nodes - halo - first, 0)
            to = first + skip - (nodes - halo)
            x_ref[to : to + part - skip, :features] = piece[part + skip : 2 * part]
    w = w_ref[...]
    ww = jnp.concatenate([w, w], axis=0)
    bias = bias_ref[...]
    hidden_width = w.shape[1]
    total = jnp.zeros((2 * features, hidden_width), F32)
    for b in range(nodes // CHUNK):
        rows = pl.ds(b * CHUNK, CHUNK)
        both = jnp.dot(adj_ref[rows, :], x_ref[...], preferred_element_type=F32)
        y = both[:, :features]
        inv = 1.0 / both[:, features:]
        inv = jnp.concatenate([inv] * (hidden_width // features), axis=1)
        y_hi = y.astype(BF16)
        y_lo = (y - y_hi.astype(F32)).astype(BF16)
        yy = jnp.concatenate([y_hi, y_lo], axis=1)
        v = jnp.dot(yy, ww, preferred_element_type=F32) * inv + bias
        v2 = v * v
        t = jnp.tanh(v * (GELU_A + (GELU_A * GELU_B) * v2))
        half = 0.5 + 0.5 * t
        h = v * half
        hidden_ref[rows, :] = h.astype(BF16)
        slope = half + h * (1.0 - t) * (GELU_A + (3.0 * GELU_A * GELU_B) * v2)
        scaled = (cot_ref[rows, :].astype(F32) * inv * slope).astype(BF16)
        total += lax.dot_general(yy, scaled, (((0,), (0,)), ((), ())), preferred_element_type=F32)
    total = total[:features] + total[features:]
    total = total.reshape(mine_ref.shape[0], CORES, width, hidden_width)
    first = core_ref[0] == 0
    mine_ref[...] = jnp.where(first, total[:, 0], total[:, 1])
    other_ref[...] = jnp.where(first, total[:, 1], total[:, 0])


def body(features, w_in, bias, tiles, tile_cols, tile_counts, cotangent):
    block_rows, slots, side, _ = tiles.shape
    n_features, hidden_width = w_in.shape
    feat_size = lax.axis_size(FEAT)
    row_size = lax.axis_size("rows")
    nodes = block_rows * side
    halo = HALO_BLK * side
    width, owners, part = features.shape
    feat_id = lax.axis_index(FEAT)
    row_id = lax.axis_index("rows")
    cycle = block_rows * row_size

    vmem = pl.BlockSpec(memory_space=pltpu.VMEM)
    smem = pl.BlockSpec(memory_space=pltpu.SMEM)
    step = jnp.where(row_id * 2 < row_size, 1, -1).reshape(1).astype(jnp.int32)
    send = pl.pallas_call(
        lambda *refs: send_kernel(*refs, ring=row_size),
        out_shape=jax.ShapeDtypeStruct((owners, width, LANES), BF16),
        in_specs=[smem, vmem],
        out_specs=vmem,
        scratch_shapes=[pltpu.VMEM((owners * width, LANES), F32)],
        compiler_params=pltpu.CompilerParams(vmem_limit_bytes=8 * 2**20),
        name="pieces",
    )(step, features.transpose(0, 2, 1))
    recv = lax.all_to_all(send, ALL, split_axis=0, concat_axis=0, tiled=True)
    recv = recv.reshape(feat_size, row_size, width, LANES)

    base = (feat_id * cycle + row_id * block_rows).reshape(1).astype(jnp.int32)
    ext = nodes + 2 * halo
    adj = pl.pallas_call(
        lambda *refs: adjacency_kernel(*refs, cycle=cycle),
        out_shape=jax.ShapeDtypeStruct((nodes, ext), BF16),
        in_specs=[smem, smem, smem, vmem],
        out_specs=vmem,
        compiler_params=pltpu.CompilerParams(vmem_limit_bytes=16 * 2**20),
        cost_estimate=pl.CostEstimate(flops=2 * 10**6, bytes_accessed=4 * 10**6, transcendentals=0),
        name="adjacency",
    )(tile_cols, tile_counts, base, tiles)
    chips = feat_size // CORES
    half = jax.ShapeDtypeStruct((chips, width, hidden_width), F32)
    hidden, mine, other = pl.pallas_call(
        layer_kernel,
        out_shape=(jax.ShapeDtypeStruct((nodes, hidden_width), BF16), half, half),
        in_specs=[vmem] * 5 + [smem],
        out_specs=(vmem, vmem, vmem),
        scratch_shapes=[pltpu.VMEM((ext, 2 * n_features), BF16)],
        compiler_params=pltpu.CompilerParams(vmem_limit_bytes=24 * 2**20),
        cost_estimate=pl.CostEstimate(flops=600 * 10**6, bytes_accessed=4 * 10**6, transcendentals=nodes * hidden_width),
        name="layer",
    )(recv, adj, w_in, bias.reshape(1, hidden_width), cotangent, lax.axis_index("core").reshape(1))

    pair = (mine + lax.ppermute(other, "core", [(0, 1), (1, 0)])).astype(BF16)
    copies = jnp.broadcast_to(pair[:, None], (chips, row_size, width, hidden_width))
    copies = copies.reshape(chips * row_size, width, hidden_width)
    pieces = lax.all_to_all(copies, ("x", "rows"), split_axis=0, concat_axis=0, tiled=True)
    return hidden, jnp.sum(pieces.astype(F32), axis=0)


def solution(mesh):
    devices = mesh.devices
    mesh = jax.sharding.Mesh(devices.reshape(devices.shape[0] // CORES, CORES, devices.shape[1]), ALL)
    in_specs = (
        P(FEAT, None, "rows"),
        P(),
        P(),
        P(ALL, None, None, None),
        P(ALL, None),
        P(ALL),
        P(ALL, None),
    )
    out_specs = (P(ALL, None), P(FEAT, None))
    return jax.shard_map(body, mesh=mesh, in_specs=in_specs, out_specs=out_specs, check_vma=False)
```

```python
import jax
import jax.numpy as jnp
from jax import lax
from jax.experimental import pallas as pl
from jax.experimental.pallas import tpu as pltpu
from jax.sharding import PartitionSpec as P

HALO_BLK = 2
LANES = 128
CORES = 2
FEAT = ("x", "core")
ALL = ("x", "core", "rows")
CHUNK = 768
GELU_A, GELU_B = 0.7978845608, 0.044715
F32 = jnp.float32
BF16 = jnp.bfloat16


def adjacency_kernel(cols_ref, counts_ref, base_ref, tiles_ref, adj_ref, *, cycle):
    nb, slots, side, _ = tiles_ref.shape
    adj_ref[...] = jnp.zeros_like(adj_ref)
    eye = (
        lax.broadcasted_iota(jnp.int32, (side, side), 0)
        == lax.broadcasted_iota(jnp.int32, (side, side), 1)
    )
    eye = jnp.where(eye, 1.0, 0.0).astype(BF16)
    base = base_ref[0]
    for b in range(nb):
        rows = pl.ds(b * side, side)
        adj_ref[rows, pl.ds((b + HALO_BLK) * side, side)] = eye
        for k in range(slots):

            @pl.when(k < counts_ref[b])
            def _():
                block = lax.rem(cols_ref[b, k] - base + HALO_BLK + cycle, cycle)
                at = (rows, pl.ds(pl.multiple_of(block * side, side), side))
                adj_ref[at] = adj_ref[at] + tiles_ref[b, k]


def send_kernel(step_ref, x_ref, out_ref, rows_ref, *, ring):
    width, part, owners = x_ref.shape
    i = lax.broadcasted_iota(jnp.int32, (owners, owners), 0)
    k = lax.broadcasted_iota(jnp.int32, (owners, owners), 1)
    beside = (i // ring) * ring + lax.rem(lax.rem(i, ring) + step_ref[0] + ring, ring)
    pick = jnp.concatenate([jnp.where(k == i, 1.0, 0.0), jnp.where(k == beside, 1.0, 0.0)], axis=1).astype(BF16)
    none = jnp.zeros((part, owners), BF16)
    rest = jnp.zeros((LANES - 2 * part, 2 * owners), BF16)
    for c in range(width):
        x = x_ref[c]
        spread = jnp.concatenate(
            [jnp.concatenate([x, none], axis=1), jnp.concatenate([none, x], axis=1), rest], axis=0
        )
        rows_ref[pl.ds(c, owners, stride=width), :] = lax.dot_general(
            pick, spread, (((1,), (1,)), ((), ())), preferred_element_type=F32
        )
    out_ref[...] = rows_ref[...].astype(BF16).reshape(out_ref.shape)


def layer_kernel(recv_ref, adj_ref, w_ref, bias_ref, cot_ref, core_ref, hidden_ref, mine_ref, other_ref, x_ref):
    groups, senders, width, lanes = recv_ref.shape
    features = groups * width
    nodes = hidden_ref.shape[0]
    ext = x_ref.shape[0]
    halo = (ext - nodes) // 2
    part = nodes // senders
    x_ref[:, features:] = jnp.ones((ext, features), BF16)
    for r in range(senders):
        piece = recv_ref[:, r].reshape(features, lanes).T
        x_ref[halo + r * part : halo + (r + 1) * part, :features] = piece[:part]
        first, last = r * part, (r + 1) * part
        if first < halo:
            n = min(last, halo) - first
            x_ref[halo + nodes + first : halo + nodes + first + n, :features] = piece[part : part + n]
        if last > nodes - halo:
            skip = max(nodes - halo - first, 0)
            to = first + skip - (nodes - halo)
            x_ref[to : to + part - skip, :features] = piece[part + skip : 2 * part]
    w = w_ref[...]
    ww = jnp.concatenate([w, w], axis=0)
    bias = bias_ref[...]
    hidden_width = w.shape[1]
    total = jnp.zeros((2 * features, hidden_width), F32)
    for b in range(nodes // CHUNK):
        rows = pl.ds(b * CHUNK, CHUNK)
        both = jnp.dot(adj_ref[rows, :], x_ref[...], preferred_element_type=F32)
        y = both[:, :features]
        inv = 1.0 / both[:, features:]
        inv = jnp.concatenate([inv] * (hidden_width // features), axis=1)
        y_hi = y.astype(BF16)
        y_lo = (y - y_hi.astype(F32)).astype(BF16)
        yy = jnp.concatenate([y_hi, y_lo], axis=1)
        v = jnp.dot(yy, ww, preferred_element_type=F32) * inv + bias
        v2 = v * v
        t = jnp.tanh(v * (GELU_A + (GELU_A * GELU_B) * v2))
        half = 0.5 + 0.5 * t
        h = v * half
        hidden_ref[rows, :] = h
        slope = half + h * (1.0 - t) * (GELU_A + (3.0 * GELU_A * GELU_B) * v2)
        scaled = (cot_ref[rows, :].astype(F32) * inv * slope).astype(BF16)
        total += lax.dot_general(yy, scaled, (((0,), (0,)), ((), ())), preferred_element_type=F32)
    total = total[:features] + total[features:]
    total = total.reshape(mine_ref.shape[0], CORES, width, hidden_width)
    first = core_ref[0] == 0
    mine_ref[...] = jnp.where(first, total[:, 0], total[:, 1])
    other_ref[...] = jnp.where(first, total[:, 1], total[:, 0])


def body(features, w_in, bias, tiles, tile_cols, tile_counts, cotangent):
    block_rows, slots, side, _ = tiles.shape
    n_features, hidden_width = w_in.shape
    feat_size = lax.axis_size(FEAT)
    row_size = lax.axis_size("rows")
    nodes = block_rows * side
    halo = HALO_BLK * side
    width, owners, part = features.shape
    feat_id = lax.axis_index(FEAT)
    row_id = lax.axis_index("rows")
    cycle = block_rows * row_size

    vmem = pl.BlockSpec(memory_space=pltpu.VMEM)
    smem = pl.BlockSpec(memory_space=pltpu.SMEM)
    step = jnp.where(row_id * 2 < row_size, 1, -1).reshape(1).astype(jnp.int32)
    send = pl.pallas_call(
        lambda *refs: send_kernel(*refs, ring=row_size),
        out_shape=jax.ShapeDtypeStruct((owners, width, LANES), BF16),
        in_specs=[smem, vmem],
        out_specs=vmem,
        scratch_shapes=[pltpu.VMEM((owners * width, LANES), F32)],
        compiler_params=pltpu.CompilerParams(vmem_limit_bytes=4 * 2**20),
        name="pieces",
    )(step, features.transpose(0, 2, 1))
    recv = lax.all_to_all(send, ALL, split_axis=0, concat_axis=0, tiled=True)
    recv = recv.reshape(feat_size, row_size, width, LANES)

    base = (feat_id * cycle + row_id * block_rows).reshape(1).astype(jnp.int32)
    ext = nodes + 2 * halo
    adj = pl.pallas_call(
        lambda *refs: adjacency_kernel(*refs, cycle=cycle),
        out_shape=jax.ShapeDtypeStruct((nodes, ext), BF16),
        in_specs=[smem, smem, smem, vmem],
        out_specs=vmem,
        compiler_params=pltpu.CompilerParams(vmem_limit_bytes=2 * 2**20),
        cost_estimate=pl.CostEstimate(flops=2 * 10**6, bytes_accessed=4 * 10**6, transcendentals=0),
        name="adjacency",
    )(tile_cols, tile_counts, base, tiles)
    chips = feat_size // CORES
    half = jax.ShapeDtypeStruct((chips, width, hidden_width), F32)
    hidden, mine, other = pl.pallas_call(
        layer_kernel,
        out_shape=(jax.ShapeDtypeStruct((nodes, hidden_width), F32), half, half),
        in_specs=[vmem] * 5 + [smem],
        out_specs=(vmem, vmem, vmem),
        scratch_shapes=[pltpu.VMEM((ext, 2 * n_features), BF16)],
        compiler_params=pltpu.CompilerParams(vmem_limit_bytes=12 * 2**20),
        cost_estimate=pl.CostEstimate(flops=600 * 10**6, bytes_accessed=4 * 10**6, transcendentals=nodes * hidden_width),
        name="layer",
    )(recv, adj, w_in, bias.reshape(1, hidden_width), cotangent, lax.axis_index("core").reshape(1))

    other = lax.ppermute(other, "core", [(0, 1), (1, 0)])
    hidden, other = lax.optimization_barrier((hidden.astype(BF16), other))
    pair = (mine + other).astype(BF16)
    copies = jnp.broadcast_to(pair[:, None], (chips, row_size, width, hidden_width))
    copies = copies.reshape(chips * row_size, width, hidden_width)
    pieces = lax.all_to_all(copies, ("x", "rows"), split_axis=0, concat_axis=0, tiled=True)
    return hidden, jnp.sum(pieces.astype(F32), axis=0)


def solution(mesh):
    devices = mesh.devices
    mesh = jax.sharding.Mesh(devices.reshape(devices.shape[0] // CORES, CORES, devices.shape[1]), ALL)
    in_specs = (
        P(FEAT, None, "rows"),
        P(),
        P(),
        P(ALL, None, None, None),
        P(ALL, None),
        P(ALL),
        P(ALL, None),
    )
    out_specs = (P(ALL, None), P(FEAT, None))
    return jax.shard_map(body, mesh=mesh, in_specs=in_specs, out_specs=out_specs, check_vma=False)
```

```python
import jax
import jax.numpy as jnp
from jax import lax
from jax.experimental import pallas as pl
from jax.experimental.pallas import tpu as pltpu
from jax.sharding import PartitionSpec as P

HALO_BLK = 2
LANES = 128
CORES = 2
PARTS = 4
FEAT = ("x", "core")
ALL = ("x", "core", "rows")
CHUNK = 768
GELU_A, GELU_B = 0.7978845608, 0.044715
F32 = jnp.float32
BF16 = jnp.bfloat16


def adjacency_kernel(cols_ref, counts_ref, base_ref, tiles_ref, w_ref, adj_ref, ww_ref, *, cycle, slices):
    features = w_ref.shape[0]
    quarter = features // slices // PARTS
    i = lax.broadcasted_iota(jnp.int32, (features, features), 0)
    k = lax.broadcasted_iota(jnp.int32, (features, features), 1)
    per = slices * quarter
    source = (lax.rem(i, per) // quarter) * (PARTS * quarter) + (i // per) * quarter + lax.rem(i, quarter)
    order = jnp.where(k == source, 1.0, 0.0).astype(BF16)
    w = jnp.dot(order, w_ref[...], preferred_element_type=F32).astype(BF16)
    ww_ref[...] = jnp.concatenate([w, w], axis=0)
    nb, slots, side, _ = tiles_ref.shape
    adj_ref[...] = jnp.zeros_like(adj_ref)
    eye = (
        lax.broadcasted_iota(jnp.int32, (side, side), 0)
        == lax.broadcasted_iota(jnp.int32, (side, side), 1)
    )
    eye = jnp.where(eye, 1.0, 0.0).astype(BF16)
    base = base_ref[0]
    for b in range(nb):
        rows = pl.ds(b * side, side)
        adj_ref[rows, pl.ds((b + HALO_BLK) * side, side)] = eye
        for k in range(slots):

            @pl.when(k < counts_ref[b])
            def _():
                block = lax.rem(cols_ref[b, k] - base + HALO_BLK + cycle, cycle)
                at = (rows, pl.ds(pl.multiple_of(block * side, side), side))
                adj_ref[at] = adj_ref[at] + tiles_ref[b, k]


def send_kernel(step_ref, x_ref, out_ref, rows_ref, *, ring):
    width, part, owners = x_ref.shape
    quarter = width // PARTS
    third = LANES - 2 * part
    i = lax.broadcasted_iota(jnp.int32, (owners, owners), 0)
    k = lax.broadcasted_iota(jnp.int32, (owners, owners), 1)
    beside = (i // ring) * ring + lax.rem(lax.rem(i, ring) + step_ref[0] + ring, ring)
    pick = jnp.concatenate([jnp.where(k == i, 1.0, 0.0), jnp.where(k == beside, 1.0, 0.0)], axis=1).astype(BF16)
    none = jnp.zeros((part, owners), BF16)

    def both(c):
        x = x_ref[c]
        return jnp.concatenate([jnp.concatenate([x, none], axis=1), jnp.concatenate([none, x], axis=1)], axis=0)

    count = owners * quarter
    for b in range(quarter):
        last = both((PARTS - 1) * quarter + b)
        for t in range(PARTS - 1):
            spread = jnp.concatenate([both(t * quarter + b), last[t * third : (t + 1) * third]], axis=0)
            rows_ref[pl.ds(t * count + b, owners, stride=quarter), :] = lax.dot_general(
                pick, spread, (((1,), (1,)), ((), ())), preferred_element_type=F32
            )
    for t in range(PARTS - 1):
        rows = rows_ref[t * count : (t + 1) * count, :].astype(BF16)
        out_ref[:, :, t * LANES : (t + 1) * LANES] = rows.reshape(owners, quarter, LANES)


def layer_kernel(recv_ref, adj_ref, ww_ref, bias_ref, cot_ref, core_ref, hidden_ref, mine_ref, other_ref, x_ref):
    groups, senders, quarter, _ = recv_ref.shape
    per = groups * quarter
    features = PARTS * per
    nodes = hidden_ref.shape[0]
    ext = x_ref.shape[0]
    halo = (ext - nodes) // 2
    part = nodes // senders
    x_ref[:, features:] = jnp.ones((ext, features), BF16)
    for r in range(senders):
        tiles = [
            recv_ref[:, r, :, t * LANES : (t + 1) * LANES].reshape(per, LANES) for t in range(PARTS - 1)
        ]
        last = [tile[:, 2 * part :] for tile in tiles] + [jnp.zeros((per, LANES - 2 * part), BF16)]
        piece = jnp.concatenate(tiles + [jnp.concatenate(last, axis=1)], axis=0).T
        x_ref[halo + r * part : halo + (r + 1) * part, :features] = piece[:part]
        first, last = r * part, (r + 1) * part
        if first < halo:
            n = min(last, halo) - first
            x_ref[halo + nodes + first : halo + nodes + first + n, :features] = piece[part : part + n]
        if last > nodes - halo:
            skip = max(nodes - halo - first, 0)
            to = first + skip - (nodes - halo)
            x_ref[to : to + part - skip, :features] = piece[part + skip : 2 * part]
    ww = ww_ref[...]
    bias = bias_ref[...]
    hidden_width = ww.shape[1]
    total = jnp.zeros((2 * features, hidden_width), F32)
    for b in range(nodes // CHUNK):
        rows = pl.ds(b * CHUNK, CHUNK)
        both = jnp.dot(adj_ref[rows, :], x_ref[...], preferred_element_type=F32)
        y = both[:, :features]
        inv = 1.0 / both[:, features:]
        inv = jnp.concatenate([inv] * (hidden_width // features), axis=1)
        y_hi = y.astype(BF16)
        y_lo = (y - y_hi.astype(F32)).astype(BF16)
        yy = jnp.concatenate([y_hi, y_lo], axis=1)
        v = jnp.dot(yy, ww, preferred_element_type=F32) * inv + bias
        v2 = v * v
        t = jnp.tanh(v * (GELU_A + (GELU_A * GELU_B) * v2))
        half = 0.5 + 0.5 * t
        h = v * half
        hidden_ref[rows, :] = h
        slope = half + h * (1.0 - t) * (GELU_A + (3.0 * GELU_A * GELU_B) * v2)
        scaled = (cot_ref[rows, :].astype(F32) * inv * slope).astype(BF16)
        total += lax.dot_general(yy, scaled, (((0,), (0,)), ((), ())), preferred_element_type=F32)
    total = total[:features] + total[features:]
    first = core_ref[0] == 0
    for chip in range(mine_ref.shape[0]):
        at = [q * per + chip * CORES * quarter for q in range(PARTS)]
        even = jnp.concatenate([total[i : i + quarter] for i in at], axis=0)
        odd = jnp.concatenate([total[i + quarter : i + 2 * quarter] for i in at], axis=0)
        mine_ref[chip] = jnp.where(first, even, odd)
        other_ref[chip] = jnp.where(first, odd, even)


def body(features, w_in, bias, tiles, tile_cols, tile_counts, cotangent):
    block_rows, slots, side, _ = tiles.shape
    n_features, hidden_width = w_in.shape
    feat_size = lax.axis_size(FEAT)
    row_size = lax.axis_size("rows")
    nodes = block_rows * side
    halo = HALO_BLK * side
    width, owners, part = features.shape
    feat_id = lax.axis_index(FEAT)
    row_id = lax.axis_index("rows")
    cycle = block_rows * row_size

    vmem = pl.BlockSpec(memory_space=pltpu.VMEM)
    smem = pl.BlockSpec(memory_space=pltpu.SMEM)
    step = jnp.where(row_id * 2 < row_size, 1, -1).reshape(1).astype(jnp.int32)
    send = pl.pallas_call(
        lambda *refs: send_kernel(*refs, ring=row_size),
        out_shape=jax.ShapeDtypeStruct((owners, width // PARTS, (PARTS - 1) * LANES), BF16),
        in_specs=[smem, vmem],
        out_specs=vmem,
        scratch_shapes=[pltpu.VMEM((owners * (width - width // PARTS), LANES), F32)],
        compiler_params=pltpu.CompilerParams(vmem_limit_bytes=4 * 2**20),
        name="pieces",
    )(step, features.transpose(0, 2, 1))
    recv = lax.all_to_all(send, ALL, split_axis=0, concat_axis=0, tiled=True)
    recv = recv.reshape(feat_size, row_size, width // PARTS, (PARTS - 1) * LANES)

    base = (feat_id * cycle + row_id * block_rows).reshape(1).astype(jnp.int32)
    ext = nodes + 2 * halo
    adj, ww = pl.pallas_call(
        lambda *refs: adjacency_kernel(*refs, cycle=cycle, slices=feat_size),
        out_shape=(
            jax.ShapeDtypeStruct((nodes, ext), BF16),
            jax.ShapeDtypeStruct((2 * n_features, hidden_width), BF16),
        ),
        in_specs=[smem, smem, smem, vmem, vmem],
        out_specs=(vmem, vmem),
        compiler_params=pltpu.CompilerParams(vmem_limit_bytes=2 * 2**20),
        cost_estimate=pl.CostEstimate(flops=2 * 10**6, bytes_accessed=4 * 10**6, transcendentals=0),
        name="adjacency",
    )(tile_cols, tile_counts, base, tiles, w_in)
    chips = feat_size // CORES
    half = jax.ShapeDtypeStruct((chips, width, hidden_width), F32)
    hidden, mine, other = pl.pallas_call(
        layer_kernel,
        out_shape=(jax.ShapeDtypeStruct((nodes, hidden_width), F32), half, half),
        in_specs=[vmem] * 5 + [smem],
        out_specs=(vmem, vmem, vmem),
        scratch_shapes=[pltpu.VMEM((ext, 2 * n_features), BF16)],
        compiler_params=pltpu.CompilerParams(vmem_limit_bytes=12 * 2**20),
        cost_estimate=pl.CostEstimate(flops=600 * 10**6, bytes_accessed=4 * 10**6, transcendentals=nodes * hidden_width),
        name="layer",
    )(recv, adj, ww, bias.reshape(1, hidden_width), cotangent, lax.axis_index("core").reshape(1))

    other = lax.ppermute(other, "core", [(0, 1), (1, 0)])
    hidden, other = lax.optimization_barrier((hidden.astype(BF16), other))
    pair = (mine + other).astype(BF16)
    copies = jnp.broadcast_to(pair[:, None], (chips, row_size, width, hidden_width))
    copies = copies.reshape(chips * row_size, width, hidden_width)
    pieces = lax.all_to_all(copies, ("x", "rows"), split_axis=0, concat_axis=0, tiled=True)
    return hidden, jnp.sum(pieces.astype(F32), axis=0)


def solution(mesh):
    devices = mesh.devices
    mesh = jax.sharding.Mesh(devices.reshape(devices.shape[0] // CORES, CORES, devices.shape[1]), ALL)
    in_specs = (
        P(FEAT, None, "rows"),
        P(),
        P(),
        P(ALL, None, None, None),
        P(ALL, None),
        P(ALL),
        P(ALL, None),
    )
    out_specs = (P(ALL, None), P(FEAT, None))
    return jax.shard_map(body, mesh=mesh, in_specs=in_specs, out_specs=out_specs, check_vma=False)
```

```python
import jax
import jax.numpy as jnp
from jax import lax
from jax.experimental import pallas as pl
from jax.experimental.pallas import tpu as pltpu
from jax.sharding import PartitionSpec as P

HALO_BLK = 2
LANES = 128
CORES = 2
PARTS = 4
COPIES = 2
FEAT = ("x", "core")
ALL = ("x", "core", "rows")
CHUNK = 768
GELU_A, GELU_B = 0.7978845608, 0.044715
F32 = jnp.float32
BF16 = jnp.bfloat16


def adjacency_kernel(cols_ref, counts_ref, base_ref, tiles_ref, w_ref, adj_ref, ww_ref, *, cycle, slices):
    features = w_ref.shape[0]
    quarter = features // slices // PARTS
    i = lax.broadcasted_iota(jnp.int32, (features, features), 0)
    k = lax.broadcasted_iota(jnp.int32, (features, features), 1)
    per = slices * quarter
    source = (lax.rem(i, per) // quarter) * (PARTS * quarter) + (i // per) * quarter + lax.rem(i, quarter)
    order = jnp.where(k == source, 1.0, 0.0).astype(BF16)
    w = jnp.dot(order, w_ref[...], preferred_element_type=F32).astype(BF16)
    ww_ref[...] = jnp.concatenate([w, w], axis=0)
    nb, slots, side, _ = tiles_ref.shape
    adj_ref[...] = jnp.zeros_like(adj_ref)
    eye = (
        lax.broadcasted_iota(jnp.int32, (side, side), 0)
        == lax.broadcasted_iota(jnp.int32, (side, side), 1)
    )
    eye = jnp.where(eye, 1.0, 0.0).astype(BF16)
    base = base_ref[0]
    for b in range(nb):
        rows = pl.ds(b * side, side)
        adj_ref[rows, pl.ds((b + HALO_BLK) * side, side)] = eye
        for k in range(slots):

            @pl.when(k < counts_ref[b])
            def _():
                block = lax.rem(cols_ref[b, k] - base + HALO_BLK + cycle, cycle)
                at = (rows, pl.ds(pl.multiple_of(block * side, side), side))
                adj_ref[at] = adj_ref[at] + tiles_ref[b, k]


def send_kernel(step_ref, x_hbm, out_hbm, x_ref, rows_ref, out_ref, load_sem, store_sem, *, ring):
    width, part, owners = x_ref.shape
    quarter = width // PARTS
    third = LANES - 2 * part
    loads = []
    for n in range(COPIES):
        at = pl.ds(n * (width // COPIES), width // COPIES)
        loads.append(pltpu.make_async_copy(x_hbm.at[at], x_ref.at[at], load_sem.at[n]))
        loads[n].start()
    i = lax.broadcasted_iota(jnp.int32, (owners, owners), 0)
    k = lax.broadcasted_iota(jnp.int32, (owners, owners), 1)
    beside = (i // ring) * ring + lax.rem(lax.rem(i, ring) + step_ref[0] + ring, ring)
    pick = jnp.concatenate([jnp.where(k == i, 1.0, 0.0), jnp.where(k == beside, 1.0, 0.0)], axis=1).astype(BF16)
    none = jnp.zeros((part, owners), BF16)
    for load in loads:
        load.wait()

    def both(c):
        x = x_ref[c]
        return jnp.concatenate([jnp.concatenate([x, none], axis=1), jnp.concatenate([none, x], axis=1)], axis=0)

    count = owners * quarter
    for b in range(quarter):
        last = both((PARTS - 1) * quarter + b)
        for t in range(PARTS - 1):
            spread = jnp.concatenate([both(t * quarter + b), last[t * third : (t + 1) * third]], axis=0)
            rows_ref[pl.ds(t * count + b, owners, stride=quarter), :] = lax.dot_general(
                pick, spread, (((1,), (1,)), ((), ())), preferred_element_type=F32
            )
    stores = []
    some = owners // COPIES
    for n in range(COPIES):
        at = pl.ds(n * some, some)
        for t in range(PARTS - 1):
            rows = rows_ref[pl.ds(t * count + n * some * quarter, some * quarter), :].astype(BF16)
            out_ref[at, :, t * LANES : (t + 1) * LANES] = rows.reshape(some, quarter, LANES)
        stores.append(pltpu.make_async_copy(out_ref.at[at], out_hbm.at[at], store_sem.at[n]))
        stores[n].start()
    for store in stores:
        store.wait()


def layer_kernel(recv_ref, adj_ref, ww_ref, bias_ref, cot_ref, core_ref, hidden_ref, mine_ref, other_ref, x_ref):
    groups, senders, quarter, _ = recv_ref.shape
    per = groups * quarter
    features = PARTS * per
    nodes = hidden_ref.shape[0]
    ext = x_ref.shape[0]
    halo = (ext - nodes) // 2
    part = nodes // senders
    x_ref[:, features:] = jnp.ones((ext, features), BF16)
    for r in range(senders):
        tiles = [
            recv_ref[:, r, :, t * LANES : (t + 1) * LANES].reshape(per, LANES) for t in range(PARTS - 1)
        ]
        last = [tile[:, 2 * part :] for tile in tiles] + [jnp.zeros((per, LANES - 2 * part), BF16)]
        piece = jnp.concatenate(tiles + [jnp.concatenate(last, axis=1)], axis=0).T
        x_ref[halo + r * part : halo + (r + 1) * part, :features] = piece[:part]
        first, last = r * part, (r + 1) * part
        if first < halo:
            n = min(last, halo) - first
            x_ref[halo + nodes + first : halo + nodes + first + n, :features] = piece[part : part + n]
        if last > nodes - halo:
            skip = max(nodes - halo - first, 0)
            to = first + skip - (nodes - halo)
            x_ref[to : to + part - skip, :features] = piece[part + skip : 2 * part]
    ww = ww_ref[...]
    bias = bias_ref[...]
    hidden_width = ww.shape[1]
    total = jnp.zeros((2 * features, hidden_width), F32)
    for b in range(nodes // CHUNK):
        rows = pl.ds(b * CHUNK, CHUNK)
        both = jnp.dot(adj_ref[rows, :], x_ref[...], preferred_element_type=F32)
        y = both[:, :features]
        inv = 1.0 / both[:, features:]
        inv = jnp.concatenate([inv] * (hidden_width // features), axis=1)
        y_hi = y.astype(BF16)
        y_lo = (y - y_hi.astype(F32)).astype(BF16)
        yy = jnp.concatenate([y_hi, y_lo], axis=1)
        v = jnp.dot(yy, ww, preferred_element_type=F32) * inv + bias
        v2 = v * v
        t = jnp.tanh(v * (GELU_A + (GELU_A * GELU_B) * v2))
        half = 0.5 + 0.5 * t
        h = v * half
        hidden_ref[rows, :] = h
        slope = half + h * (1.0 - t) * (GELU_A + (3.0 * GELU_A * GELU_B) * v2)
        scaled = (cot_ref[rows, :].astype(F32) * inv * slope).astype(BF16)
        total += lax.dot_general(yy, scaled, (((0,), (0,)), ((), ())), preferred_element_type=F32)
    total = total[:features] + total[features:]
    first = core_ref[0] == 0
    for chip in range(mine_ref.shape[0]):
        at = [q * per + chip * CORES * quarter for q in range(PARTS)]
        even = jnp.concatenate([total[i : i + quarter] for i in at], axis=0)
        odd = jnp.concatenate([total[i + quarter : i + 2 * quarter] for i in at], axis=0)
        mine_ref[chip] = jnp.where(first, even, odd)
        other_ref[chip] = jnp.where(first, odd, even)


def body(features, w_in, bias, tiles, tile_cols, tile_counts, cotangent):
    block_rows, slots, side, _ = tiles.shape
    n_features, hidden_width = w_in.shape
    feat_size = lax.axis_size(FEAT)
    row_size = lax.axis_size("rows")
    nodes = block_rows * side
    halo = HALO_BLK * side
    width, owners, part = features.shape
    feat_id = lax.axis_index(FEAT)
    row_id = lax.axis_index("rows")
    cycle = block_rows * row_size

    vmem = pl.BlockSpec(memory_space=pltpu.VMEM)
    smem = pl.BlockSpec(memory_space=pltpu.SMEM)
    step = jnp.where(row_id * 2 < row_size, 1, -1).reshape(1).astype(jnp.int32)
    hbm = pl.BlockSpec(memory_space=pltpu.MemorySpace.HBM)
    sent = (owners, width // PARTS, (PARTS - 1) * LANES)
    send = pl.pallas_call(
        lambda *refs: send_kernel(*refs, ring=row_size),
        out_shape=jax.ShapeDtypeStruct(sent, BF16),
        in_specs=[smem, hbm],
        out_specs=hbm,
        scratch_shapes=[
            pltpu.VMEM((width, part, owners), BF16),
            pltpu.VMEM((owners * (width - width // PARTS), LANES), F32),
            pltpu.VMEM(sent, BF16),
            pltpu.SemaphoreType.DMA((COPIES,)),
            pltpu.SemaphoreType.DMA((COPIES,)),
        ],
        compiler_params=pltpu.CompilerParams(vmem_limit_bytes=4 * 2**20),
        name="pieces",
    )(step, pltpu.with_memory_space_constraint(features.transpose(0, 2, 1), pltpu.MemorySpace.HBM))
    recv = lax.all_to_all(send, ALL, split_axis=0, concat_axis=0, tiled=True)
    recv = recv.reshape(feat_size, row_size, width // PARTS, (PARTS - 1) * LANES)

    base = (feat_id * cycle + row_id * block_rows).reshape(1).astype(jnp.int32)
    ext = nodes + 2 * halo
    adj, ww = pl.pallas_call(
        lambda *refs: adjacency_kernel(*refs, cycle=cycle, slices=feat_size),
        out_shape=(
            jax.ShapeDtypeStruct((nodes, ext), BF16),
            jax.ShapeDtypeStruct((2 * n_features, hidden_width), BF16),
        ),
        in_specs=[smem, smem, smem, vmem, vmem],
        out_specs=(vmem, vmem),
        compiler_params=pltpu.CompilerParams(vmem_limit_bytes=2 * 2**20),
        cost_estimate=pl.CostEstimate(flops=2 * 10**6, bytes_accessed=4 * 10**6, transcendentals=0),
        name="adjacency",
    )(tile_cols, tile_counts, base, tiles, w_in)
    chips = feat_size // CORES
    half = jax.ShapeDtypeStruct((chips, width, hidden_width), F32)
    hidden, mine, other = pl.pallas_call(
        layer_kernel,
        out_shape=(jax.ShapeDtypeStruct((nodes, hidden_width), F32), half, half),
        in_specs=[vmem] * 5 + [smem],
        out_specs=(vmem, vmem, vmem),
        scratch_shapes=[pltpu.VMEM((ext, 2 * n_features), BF16)],
        compiler_params=pltpu.CompilerParams(vmem_limit_bytes=12 * 2**20),
        cost_estimate=pl.CostEstimate(flops=600 * 10**6, bytes_accessed=4 * 10**6, transcendentals=nodes * hidden_width),
        name="layer",
    )(recv, adj, ww, bias.reshape(1, hidden_width), cotangent, lax.axis_index("core").reshape(1))

    other = lax.ppermute(other, "core", [(0, 1), (1, 0)])
    hidden, other = lax.optimization_barrier((hidden.astype(BF16), other))
    pair = (mine + other).astype(BF16)
    copies = jnp.broadcast_to(pair[:, None], (chips, row_size, width, hidden_width))
    copies = copies.reshape(chips * row_size, width, hidden_width)
    pieces = lax.all_to_all(copies, ("x", "rows"), split_axis=0, concat_axis=0, tiled=True)
    return hidden, jnp.sum(pieces.astype(F32), axis=0)


def solution(mesh):
    devices = mesh.devices
    mesh = jax.sharding.Mesh(devices.reshape(devices.shape[0] // CORES, CORES, devices.shape[1]), ALL)
    in_specs = (
        P(FEAT, None, "rows"),
        P(),
        P(),
        P(ALL, None, None, None),
        P(ALL, None),
        P(ALL),
        P(ALL, None),
    )
    out_specs = (P(ALL, None), P(FEAT, None))
    return jax.shard_map(body, mesh=mesh, in_specs=in_specs, out_specs=out_specs, check_vma=False)
```

```python
import jax
import jax.numpy as jnp
from jax import lax
from jax.experimental import pallas as pl
from jax.experimental.pallas import tpu as pltpu
from jax.sharding import PartitionSpec as P

HALO_BLK = 2
LANES = 128
CORES = 2
PARTS = 4
FEAT = ("x", "core")
ALL = ("x", "core", "rows")
CHUNK = 768
GELU_A, GELU_B = 0.7978845608, 0.044715
F32 = jnp.float32
BF16 = jnp.bfloat16


def adjacency_kernel(cols_ref, counts_ref, base_ref, tiles_ref, adj_ref, *, cycle):
    nb, slots, side, _ = tiles_ref.shape
    adj_ref[...] = jnp.zeros_like(adj_ref)
    eye = (
        lax.broadcasted_iota(jnp.int32, (side, side), 0)
        == lax.broadcasted_iota(jnp.int32, (side, side), 1)
    )
    eye = jnp.where(eye, 1.0, 0.0).astype(BF16)
    base = base_ref[0]
    for b in range(nb):
        rows = pl.ds(b * side, side)
        adj_ref[rows, pl.ds((b + HALO_BLK) * side, side)] = eye
        for k in range(slots):

            @pl.when(k < counts_ref[b])
            def _():
                block = lax.rem(cols_ref[b, k] - base + HALO_BLK + cycle, cycle)
                at = (rows, pl.ds(pl.multiple_of(block * side, side), side))
                adj_ref[at] = adj_ref[at] + tiles_ref[b, k]


def send_kernel(step_ref, x_ref, out_ref, rows_ref, *, ring):
    width, part, owners = x_ref.shape
    quarter = width // PARTS
    third = LANES - 2 * part
    i = lax.broadcasted_iota(jnp.int32, (owners, owners), 0)
    k = lax.broadcasted_iota(jnp.int32, (owners, owners), 1)
    beside = (i // ring) * ring + lax.rem(lax.rem(i, ring) + step_ref[0] + ring, ring)
    pick = jnp.concatenate([jnp.where(k == i, 1.0, 0.0), jnp.where(k == beside, 1.0, 0.0)], axis=1).astype(BF16)
    none = jnp.zeros((part, owners), BF16)

    def both(c):
        x = x_ref[c]
        return jnp.concatenate([jnp.concatenate([x, none], axis=1), jnp.concatenate([none, x], axis=1)], axis=0)

    count = owners * quarter
    for b in range(quarter):
        last = both((PARTS - 1) * quarter + b)
        for t in range(PARTS - 1):
            spread = jnp.concatenate([both(t * quarter + b), last[t * third : (t + 1) * third]], axis=0)
            rows_ref[pl.ds(t * count + b, owners, stride=quarter), :] = lax.dot_general(
                pick, spread, (((1,), (1,)), ((), ())), preferred_element_type=F32
            )
    for t in range(PARTS - 1):
        rows = rows_ref[t * count : (t + 1) * count, :].astype(BF16)
        out_ref[:, :, t * LANES : (t + 1) * LANES] = rows.reshape(owners, quarter, LANES)


def layer_kernel(
    recv_ref, adj_ref, w_hbm, bias_ref, cot_ref, core_ref, hidden_ref, mine_ref, other_ref, x_ref, w_ref, load_sem
):
    groups, senders, quarter, _ = recv_ref.shape
    per = groups * quarter
    features = PARTS * per
    nodes = hidden_ref.shape[0]
    ext = x_ref.shape[0]
    halo = (ext - nodes) // 2
    part = nodes // senders
    load = pltpu.make_async_copy(w_hbm, w_ref, load_sem)
    load.start()
    x_ref[:, features:] = jnp.ones((ext, features), BF16)
    for r in range(senders):
        tiles = [
            recv_ref[:, r, :, t * LANES : (t + 1) * LANES].reshape(per, LANES) for t in range(PARTS - 1)
        ]
        last = [tile[:, 2 * part :] for tile in tiles] + [jnp.zeros((per, LANES - 2 * part), BF16)]
        piece = jnp.concatenate(tiles + [jnp.concatenate(last, axis=1)], axis=0).T
        x_ref[halo + r * part : halo + (r + 1) * part, :features] = piece[:part]
        first, last = r * part, (r + 1) * part
        if first < halo:
            n = min(last, halo) - first
            x_ref[halo + nodes + first : halo + nodes + first + n, :features] = piece[part : part + n]
        if last > nodes - halo:
            skip = max(nodes - halo - first, 0)
            to = first + skip - (nodes - halo)
            x_ref[to : to + part - skip, :features] = piece[part + skip : 2 * part]
    i = lax.broadcasted_iota(jnp.int32, (features, features), 0)
    k = lax.broadcasted_iota(jnp.int32, (features, features), 1)
    source = (lax.rem(i, per) // quarter) * (PARTS * quarter) + (i // per) * quarter + lax.rem(i, quarter)
    order = jnp.where(k == source, 1.0, 0.0).astype(BF16)
    load.wait()
    w = jnp.dot(order, w_ref[...], preferred_element_type=F32).astype(BF16)
    ww = jnp.concatenate([w, w], axis=0)
    bias = bias_ref[...]
    hidden_width = ww.shape[1]
    total = jnp.zeros((2 * features, hidden_width), F32)
    for b in range(nodes // CHUNK):
        rows = pl.ds(b * CHUNK, CHUNK)
        both = jnp.dot(adj_ref[rows, :], x_ref[...], preferred_element_type=F32)
        y = both[:, :features]
        inv = 1.0 / both[:, features:]
        inv = jnp.concatenate([inv] * (hidden_width // features), axis=1)
        y_hi = y.astype(BF16)
        y_lo = (y - y_hi.astype(F32)).astype(BF16)
        yy = jnp.concatenate([y_hi, y_lo], axis=1)
        v = jnp.dot(yy, ww, preferred_element_type=F32) * inv + bias
        v2 = v * v
        t = jnp.tanh(v * (GELU_A + (GELU_A * GELU_B) * v2))
        half = 0.5 + 0.5 * t
        h = v * half
        hidden_ref[rows, :] = h
        slope = half + h * (1.0 - t) * (GELU_A + (3.0 * GELU_A * GELU_B) * v2)
        scaled = (cot_ref[rows, :].astype(F32) * inv * slope).astype(BF16)
        total += lax.dot_general(yy, scaled, (((0,), (0,)), ((), ())), preferred_element_type=F32)
    total = total[:features] + total[features:]
    first = core_ref[0] == 0
    for chip in range(mine_ref.shape[0]):
        at = [q * per + chip * CORES * quarter for q in range(PARTS)]
        even = jnp.concatenate([total[i : i + quarter] for i in at], axis=0)
        odd = jnp.concatenate([total[i + quarter : i + 2 * quarter] for i in at], axis=0)
        mine_ref[chip] = jnp.where(first, even, odd)
        other_ref[chip] = jnp.where(first, odd, even)


def body(features, w_in, bias, tiles, tile_cols, tile_counts, cotangent):
    block_rows, slots, side, _ = tiles.shape
    n_features, hidden_width = w_in.shape
    feat_size = lax.axis_size(FEAT)
    row_size = lax.axis_size("rows")
    nodes = block_rows * side
    halo = HALO_BLK * side
    width, owners, part = features.shape
    feat_id = lax.axis_index(FEAT)
    row_id = lax.axis_index("rows")
    cycle = block_rows * row_size

    vmem = pl.BlockSpec(memory_space=pltpu.VMEM)
    smem = pl.BlockSpec(memory_space=pltpu.SMEM)
    step = jnp.where(row_id * 2 < row_size, 1, -1).reshape(1).astype(jnp.int32)
    send = pl.pallas_call(
        lambda *refs: send_kernel(*refs, ring=row_size),
        out_shape=jax.ShapeDtypeStruct((owners, width // PARTS, (PARTS - 1) * LANES), BF16),
        in_specs=[smem, vmem],
        out_specs=vmem,
        scratch_shapes=[pltpu.VMEM((owners * (width - width // PARTS), LANES), F32)],
        compiler_params=pltpu.CompilerParams(vmem_limit_bytes=3 * 2**20),
        name="pieces",
    )(step, features.transpose(0, 2, 1))
    recv = lax.all_to_all(send, ALL, split_axis=0, concat_axis=0, tiled=True)
    recv = recv.reshape(feat_size, row_size, width // PARTS, (PARTS - 1) * LANES)

    base = (feat_id * cycle + row_id * block_rows).reshape(1).astype(jnp.int32)
    ext = nodes + 2 * halo
    adj = pl.pallas_call(
        lambda *refs: adjacency_kernel(*refs, cycle=cycle),
        out_shape=jax.ShapeDtypeStruct((nodes, ext), BF16),
        in_specs=[smem, smem, smem, vmem],
        out_specs=vmem,
        compiler_params=pltpu.CompilerParams(vmem_limit_bytes=2 * 2**20),
        cost_estimate=pl.CostEstimate(flops=2 * 10**6, bytes_accessed=4 * 10**6, transcendentals=0),
        name="adjacency",
    )(tile_cols, tile_counts, base, tiles)
    chips = feat_size // CORES
    half = jax.ShapeDtypeStruct((chips, width, hidden_width), F32)
    hidden, mine, other = pl.pallas_call(
        layer_kernel,
        out_shape=(jax.ShapeDtypeStruct((nodes, hidden_width), F32), half, half),
        in_specs=[vmem, vmem, pl.BlockSpec(memory_space=pltpu.MemorySpace.HBM), vmem, vmem, smem],
        out_specs=(vmem, vmem, vmem),
        scratch_shapes=[
            pltpu.VMEM((ext, 2 * n_features), BF16),
            pltpu.VMEM((n_features, hidden_width), BF16),
            pltpu.SemaphoreType.DMA,
        ],
        compiler_params=pltpu.CompilerParams(vmem_limit_bytes=3 * 2**20),
        cost_estimate=pl.CostEstimate(flops=600 * 10**6, bytes_accessed=4 * 10**6, transcendentals=nodes * hidden_width),
        name="layer",
    )(recv, adj, pltpu.with_memory_space_constraint(w_in, pltpu.MemorySpace.HBM), bias.reshape(1, hidden_width), cotangent, lax.axis_index("core").reshape(1))

    other = lax.ppermute(other, "core", [(0, 1), (1, 0)])
    pair = (mine + other).astype(BF16)
    copies = jnp.broadcast_to(pair[:, None], (chips, row_size, width, hidden_width))
    copies = copies.reshape(chips * row_size, width, hidden_width)
    pieces = lax.all_to_all(copies, ("x", "rows"), split_axis=0, concat_axis=0, tiled=True)
    return hidden.astype(BF16), jnp.sum(pieces.astype(F32), axis=0)


def solution(mesh):
    devices = mesh.devices
    mesh = jax.sharding.Mesh(devices.reshape(devices.shape[0] // CORES, CORES, devices.shape[1]), ALL)
    in_specs = (
        P(FEAT, None, "rows"),
        P(),
        P(),
        P(ALL, None, None, None),
        P(ALL, None),
        P(ALL),
        P(ALL, None),
    )
    out_specs = (P(ALL, None), P(FEAT, None))
    return jax.shard_map(body, mesh=mesh, in_specs=in_specs, out_specs=out_specs, check_vma=False)
```

```python
import jax
import jax.numpy as jnp
from jax import lax
from jax.experimental import pallas as pl
from jax.experimental.pallas import tpu as pltpu
from jax.sharding import PartitionSpec as P

HALO_BLK = 2
LANES = 128
CORES = 2
PARTS = 4
COPIES = 2
FEAT = ("x", "core")
ALL = ("x", "core", "rows")
CHUNK = 768
GELU_A, GELU_B = 0.7978845608, 0.044715
F32 = jnp.float32
BF16 = jnp.bfloat16


def adjacency_kernel(cols_ref, counts_ref, base_ref, tiles_ref, w_ref, adj_ref, ww_ref, *, cycle, slices):
    features = w_ref.shape[0]
    quarter = features // slices // PARTS
    i = lax.broadcasted_iota(jnp.int32, (features, features), 0)
    k = lax.broadcasted_iota(jnp.int32, (features, features), 1)
    per = slices * quarter
    source = (lax.rem(i, per) // quarter) * (PARTS * quarter) + (i // per) * quarter + lax.rem(i, quarter)
    order = jnp.where(k == source, 1.0, 0.0).astype(BF16)
    w = jnp.dot(order, w_ref[...], preferred_element_type=F32).astype(BF16)
    ww_ref[...] = jnp.concatenate([w, w], axis=0)
    nb, slots, side, _ = tiles_ref.shape
    adj_ref[...] = jnp.zeros_like(adj_ref)
    eye = (
        lax.broadcasted_iota(jnp.int32, (side, side), 0)
        == lax.broadcasted_iota(jnp.int32, (side, side), 1)
    )
    eye = jnp.where(eye, 1.0, 0.0).astype(BF16)
    base = base_ref[0]
    for b in range(nb):
        rows = pl.ds(b * side, side)
        adj_ref[rows, pl.ds((b + HALO_BLK) * side, side)] = eye
        for k in range(slots):

            @pl.when(k < counts_ref[b])
            def _():
                block = lax.rem(cols_ref[b, k] - base + HALO_BLK + cycle, cycle)
                at = (rows, pl.ds(pl.multiple_of(block * side, side), side))
                adj_ref[at] = adj_ref[at] + tiles_ref[b, k]


def send_kernel(step_ref, x_ref, out_hbm, rows_ref, out_ref, store_sem, *, ring):
    width, part, owners = x_ref.shape
    quarter = width // PARTS
    third = LANES - 2 * part
    i = lax.broadcasted_iota(jnp.int32, (owners, owners), 0)
    k = lax.broadcasted_iota(jnp.int32, (owners, owners), 1)
    beside = (i // ring) * ring + lax.rem(lax.rem(i, ring) + step_ref[0] + ring, ring)
    pick = jnp.concatenate([jnp.where(k == i, 1.0, 0.0), jnp.where(k == beside, 1.0, 0.0)], axis=1).astype(BF16)
    none = jnp.zeros((part, owners), BF16)

    def both(c):
        x = x_ref[c]
        return jnp.concatenate([jnp.concatenate([x, none], axis=1), jnp.concatenate([none, x], axis=1)], axis=0)

    count = owners * quarter
    for b in range(quarter):
        last = both((PARTS - 1) * quarter + b)
        for t in range(PARTS - 1):
            spread = jnp.concatenate([both(t * quarter + b), last[t * third : (t + 1) * third]], axis=0)
            rows_ref[pl.ds(t * count + b, owners, stride=quarter), :] = lax.dot_general(
                pick, spread, (((1,), (1,)), ((), ())), preferred_element_type=F32
            )
    stores = []
    some = owners // COPIES
    for n in range(COPIES):
        at = pl.ds(n * some, some)
        for t in range(PARTS - 1):
            rows = rows_ref[pl.ds(t * count + n * some * quarter, some * quarter), :].astype(BF16)
            out_ref[at, :, t * LANES : (t + 1) * LANES] = rows.reshape(some, quarter, LANES)
        stores.append(pltpu.make_async_copy(out_ref.at[at], out_hbm.at[at], store_sem.at[n]))
        stores[n].start()
    for store in stores:
        store.wait()


def layer_kernel(recv_ref, adj_ref, ww_ref, bias_ref, cot_ref, core_ref, hidden_ref, mine_ref, other_ref, x_ref):
    groups, senders, quarter, _ = recv_ref.shape
    per = groups * quarter
    features = PARTS * per
    nodes = hidden_ref.shape[0]
    ext = x_ref.shape[0]
    halo = (ext - nodes) // 2
    part = nodes // senders
    x_ref[:, features:] = jnp.ones((ext, features), BF16)
    for r in range(senders):
        tiles = [
            recv_ref[:, r, :, t * LANES : (t + 1) * LANES].reshape(per, LANES) for t in range(PARTS - 1)
        ]
        last = [tile[:, 2 * part :] for tile in tiles] + [jnp.zeros((per, LANES - 2 * part), BF16)]
        piece = jnp.concatenate(tiles + [jnp.concatenate(last, axis=1)], axis=0).T
        x_ref[halo + r * part : halo + (r + 1) * part, :features] = piece[:part]
        first, last = r * part, (r + 1) * part
        if first < halo:
            n = min(last, halo) - first
            x_ref[halo + nodes + first : halo + nodes + first + n, :features] = piece[part : part + n]
        if last > nodes - halo:
            skip = max(nodes - halo - first, 0)
            to = first + skip - (nodes - halo)
            x_ref[to : to + part - skip, :features] = piece[part + skip : 2 * part]
    ww = ww_ref[...]
    bias = bias_ref[...]
    hidden_width = ww.shape[1]
    total = jnp.zeros((2 * features, hidden_width), F32)
    for b in range(nodes // CHUNK):
        rows = pl.ds(b * CHUNK, CHUNK)
        both = jnp.dot(adj_ref[rows, :], x_ref[...], preferred_element_type=F32)
        y = both[:, :features]
        inv = 1.0 / both[:, features:]
        inv = jnp.concatenate([inv] * (hidden_width // features), axis=1)
        y_hi = y.astype(BF16)
        y_lo = (y - y_hi.astype(F32)).astype(BF16)
        yy = jnp.concatenate([y_hi, y_lo], axis=1)
        v = jnp.dot(yy, ww, preferred_element_type=F32) * inv + bias
        v2 = v * v
        t = jnp.tanh(v * (GELU_A + (GELU_A * GELU_B) * v2))
        half = 0.5 + 0.5 * t
        h = v * half
        hidden_ref[rows, :] = h
        slope = half + h * (1.0 - t) * (GELU_A + (3.0 * GELU_A * GELU_B) * v2)
        scaled = (cot_ref[rows, :].astype(F32) * inv * slope).astype(BF16)
        total += lax.dot_general(yy, scaled, (((0,), (0,)), ((), ())), preferred_element_type=F32)
    total = total[:features] + total[features:]
    first = core_ref[0] == 0
    for chip in range(mine_ref.shape[0]):
        at = [q * per + chip * CORES * quarter for q in range(PARTS)]
        even = jnp.concatenate([total[i : i + quarter] for i in at], axis=0)
        odd = jnp.concatenate([total[i + quarter : i + 2 * quarter] for i in at], axis=0)
        mine_ref[chip] = jnp.where(first, even, odd)
        other_ref[chip] = jnp.where(first, odd, even)


def body(features, w_in, bias, tiles, tile_cols, tile_counts, cotangent):
    block_rows, slots, side, _ = tiles.shape
    n_features, hidden_width = w_in.shape
    feat_size = lax.axis_size(FEAT)
    row_size = lax.axis_size("rows")
    nodes = block_rows * side
    halo = HALO_BLK * side
    width, owners, part = features.shape
    feat_id = lax.axis_index(FEAT)
    row_id = lax.axis_index("rows")
    cycle = block_rows * row_size

    vmem = pl.BlockSpec(memory_space=pltpu.VMEM)
    smem = pl.BlockSpec(memory_space=pltpu.SMEM)
    step = jnp.where(row_id * 2 < row_size, 1, -1).reshape(1).astype(jnp.int32)
    sent = (owners, width // PARTS, (PARTS - 1) * LANES)
    send = pl.pallas_call(
        lambda *refs: send_kernel(*refs, ring=row_size),
        out_shape=jax.ShapeDtypeStruct(sent, BF16),
        in_specs=[smem, vmem],
        out_specs=pl.BlockSpec(memory_space=pltpu.MemorySpace.HBM),
        scratch_shapes=[
            pltpu.VMEM((owners * (width - width // PARTS), LANES), F32),
            pltpu.VMEM(sent, BF16),
            pltpu.SemaphoreType.DMA((COPIES,)),
        ],
        compiler_params=pltpu.CompilerParams(vmem_limit_bytes=4 * 2**20),
        name="pieces",
    )(step, features.transpose(0, 2, 1))
    recv = lax.all_to_all(send, ALL, split_axis=0, concat_axis=0, tiled=True)
    recv = recv.reshape(feat_size, row_size, width // PARTS, (PARTS - 1) * LANES)

    base = (feat_id * cycle + row_id * block_rows).reshape(1).astype(jnp.int32)
    ext = nodes + 2 * halo
    adj, ww = pl.pallas_call(
        lambda *refs: adjacency_kernel(*refs, cycle=cycle, slices=feat_size),
        out_shape=(
            jax.ShapeDtypeStruct((nodes, ext), BF16),
            jax.ShapeDtypeStruct((2 * n_features, hidden_width), BF16),
        ),
        in_specs=[smem, smem, smem, vmem, vmem],
        out_specs=(vmem, vmem),
        compiler_params=pltpu.CompilerParams(vmem_limit_bytes=2 * 2**20),
        cost_estimate=pl.CostEstimate(flops=2 * 10**6, bytes_accessed=4 * 10**6, transcendentals=0),
        name="adjacency",
    )(tile_cols, tile_counts, base, tiles, w_in)
    chips = feat_size // CORES
    half = jax.ShapeDtypeStruct((chips, width, hidden_width), F32)
    hidden, mine, other = pl.pallas_call(
        layer_kernel,
        out_shape=(jax.ShapeDtypeStruct((nodes, hidden_width), F32), half, half),
        in_specs=[vmem] * 5 + [smem],
        out_specs=(vmem, vmem, vmem),
        scratch_shapes=[pltpu.VMEM((ext, 2 * n_features), BF16)],
        compiler_params=pltpu.CompilerParams(vmem_limit_bytes=12 * 2**20),
        cost_estimate=pl.CostEstimate(flops=600 * 10**6, bytes_accessed=4 * 10**6, transcendentals=nodes * hidden_width),
        name="layer",
    )(recv, adj, ww, bias.reshape(1, hidden_width), cotangent, lax.axis_index("core").reshape(1))

    other = lax.ppermute(other, "core", [(0, 1), (1, 0)])
    hidden, other = lax.optimization_barrier((hidden.astype(BF16), other))
    pair = (mine + other).astype(BF16)
    copies = jnp.broadcast_to(pair[:, None], (chips, row_size, width, hidden_width))
    copies = copies.reshape(chips * row_size, width, hidden_width)
    pieces = lax.all_to_all(copies, ("x", "rows"), split_axis=0, concat_axis=0, tiled=True)
    return hidden, jnp.sum(pieces.astype(F32), axis=0)


def solution(mesh):
    devices = mesh.devices
    mesh = jax.sharding.Mesh(devices.reshape(devices.shape[0] // CORES, CORES, devices.shape[1]), ALL)
    in_specs = (
        P(FEAT, None, "rows"),
        P(),
        P(),
        P(ALL, None, None, None),
        P(ALL, None),
        P(ALL),
        P(ALL, None),
    )
    out_specs = (P(ALL, None), P(FEAT, None))
    return jax.shard_map(body, mesh=mesh, in_specs=in_specs, out_specs=out_specs, check_vma=False)
```

```python
import jax
import jax.numpy as jnp
from jax import lax
from jax.experimental import pallas as pl
from jax.experimental.pallas import tpu as pltpu
from jax.sharding import PartitionSpec as P

HALO_BLK = 2
LANES = 128
CORES = 2
PARTS = 4
FEAT = ("x", "core")
ALL = ("x", "core", "rows")
CHUNK = 768
GELU_A, GELU_B = 0.7978845608, 0.044715
F32 = jnp.float32
BF16 = jnp.bfloat16


def adjacency_kernel(cols_ref, counts_ref, base_ref, tiles_ref, w_ref, adj_ref, ww_ref, *, cycle, slices):
    features = w_ref.shape[0]
    quarter = features // slices // PARTS
    i = lax.broadcasted_iota(jnp.int32, (features, features), 0)
    k = lax.broadcasted_iota(jnp.int32, (features, features), 1)
    per = slices * quarter
    source = (lax.rem(i, per) // quarter) * (PARTS * quarter) + (i // per) * quarter + lax.rem(i, quarter)
    order = jnp.where(k == source, 1.0, 0.0).astype(BF16)
    w = jnp.dot(order, w_ref[...], preferred_element_type=F32).astype(BF16)
    ww_ref[...] = jnp.concatenate([w, w], axis=0)
    nb, slots, side, _ = tiles_ref.shape
    adj_ref[...] = jnp.zeros_like(adj_ref)
    eye = (
        lax.broadcasted_iota(jnp.int32, (side, side), 0)
        == lax.broadcasted_iota(jnp.int32, (side, side), 1)
    )
    eye = jnp.where(eye, 1.0, 0.0).astype(BF16)
    base = base_ref[0]
    for b in range(nb):
        rows = pl.ds(b * side, side)
        adj_ref[rows, pl.ds((b + HALO_BLK) * side, side)] = eye
        for k in range(slots):

            @pl.when(k < counts_ref[b])
            def _():
                block = lax.rem(cols_ref[b, k] - base + HALO_BLK + cycle, cycle)
                at = (rows, pl.ds(pl.multiple_of(block * side, side), side))
                adj_ref[at] = adj_ref[at] + tiles_ref[b, k]


def send_kernel(step_ref, x_ref, out_ref, rows_ref, *, ring):
    width, part, owners = x_ref.shape
    quarter = width // PARTS
    third = LANES - 2 * part
    i = lax.broadcasted_iota(jnp.int32, (owners, owners), 0)
    k = lax.broadcasted_iota(jnp.int32, (owners, owners), 1)
    beside = (i // ring) * ring + lax.rem(lax.rem(i, ring) + step_ref[0] + ring, ring)
    pick = jnp.concatenate([jnp.where(k == i, 1.0, 0.0), jnp.where(k == beside, 1.0, 0.0)], axis=1).astype(BF16)
    none = jnp.zeros((part, owners), BF16)

    def both(c):
        x = x_ref[c]
        return jnp.concatenate([jnp.concatenate([x, none], axis=1), jnp.concatenate([none, x], axis=1)], axis=0)

    count = owners * quarter
    for b in range(quarter):
        last = both((PARTS - 1) * quarter + b)
        for t in range(PARTS - 1):
            spread = jnp.concatenate([both(t * quarter + b), last[t * third : (t + 1) * third]], axis=0)
            rows_ref[pl.ds(t * count + b, owners, stride=quarter), :] = lax.dot_general(
                pick, spread, (((1,), (1,)), ((), ())), preferred_element_type=F32
            )
    for t in range(PARTS - 1):
        rows = rows_ref[t * count : (t + 1) * count, :].astype(BF16)
        out_ref[:, :, t * LANES : (t + 1) * LANES] = rows.reshape(owners, quarter, LANES)


def layer_kernel(recv_ref, adj_ref, ww_ref, bias_ref, cot_ref, core_ref, hidden_ref, mine_ref, other_ref, x_ref):
    groups, senders, quarter, _ = recv_ref.shape
    per = groups * quarter
    features = PARTS * per
    nodes = hidden_ref.shape[0]
    ext = x_ref.shape[0]
    halo = (ext - nodes) // 2
    part = nodes // senders
    x_ref[:, features:] = jnp.ones((ext, features), BF16)
    for r in range(senders):
        tiles = [
            recv_ref[:, r, :, t * LANES : (t + 1) * LANES].reshape(per, LANES) for t in range(PARTS - 1)
        ]
        last = [tile[:, 2 * part :] for tile in tiles] + [jnp.zeros((per, LANES - 2 * part), BF16)]
        piece = jnp.concatenate(tiles + [jnp.concatenate(last, axis=1)], axis=0).T
        x_ref[halo + r * part : halo + (r + 1) * part, :features] = piece[:part]
        first, last = r * part, (r + 1) * part
        if first < halo:
            n = min(last, halo) - first
            x_ref[halo + nodes + first : halo + nodes + first + n, :features] = piece[part : part + n]
        if last > nodes - halo:
            skip = max(nodes - halo - first, 0)
            to = first + skip - (nodes - halo)
            x_ref[to : to + part - skip, :features] = piece[part + skip : 2 * part]
    ww = ww_ref[...]
    bias = bias_ref[...]
    hidden_width = ww.shape[1]
    total = jnp.zeros((2 * features, hidden_width), F32)
    for b in range(nodes // CHUNK):
        rows = pl.ds(b * CHUNK, CHUNK)
        both = jnp.dot(adj_ref[rows, :], x_ref[...], preferred_element_type=F32)
        y = both[:, :features]
        inv = 1.0 / both[:, features:]
        inv = jnp.concatenate([inv] * (hidden_width // features), axis=1)
        y_hi = y.astype(BF16)
        y_lo = (y - y_hi.astype(F32)).astype(BF16)
        yy = jnp.concatenate([y_hi, y_lo], axis=1)
        v = jnp.dot(yy, ww, preferred_element_type=F32) * inv + bias
        v2 = v * v
        t = jnp.tanh(v * (GELU_A + (GELU_A * GELU_B) * v2))
        half = 0.5 + 0.5 * t
        h = v * half
        hidden_ref[rows, :] = h
        slope = half + h * (1.0 - t) * (GELU_A + (3.0 * GELU_A * GELU_B) * v2)
        scaled = (cot_ref[rows, :].astype(F32) * inv * slope).astype(BF16)
        total += lax.dot_general(yy, scaled, (((0,), (0,)), ((), ())), preferred_element_type=F32)
    total = total[:features] + total[features:]
    first = core_ref[0] == 0
    for chip in range(mine_ref.shape[0]):
        at = [q * per + chip * CORES * quarter for q in range(PARTS)]
        even = jnp.concatenate([total[i : i + quarter] for i in at], axis=0)
        odd = jnp.concatenate([total[i + quarter : i + 2 * quarter] for i in at], axis=0)
        mine_ref[chip] = jnp.where(first, even, odd)
        other_ref[chip] = jnp.where(first, odd, even)


def body(features, w_in, bias, tiles, tile_cols, tile_counts, cotangent):
    block_rows, slots, side, _ = tiles.shape
    n_features, hidden_width = w_in.shape
    feat_size = lax.axis_size(FEAT)
    row_size = lax.axis_size("rows")
    nodes = block_rows * side
    halo = HALO_BLK * side
    width, owners, part = features.shape
    feat_id = lax.axis_index(FEAT)
    row_id = lax.axis_index("rows")
    cycle = block_rows * row_size

    vmem = pl.BlockSpec(memory_space=pltpu.VMEM)
    smem = pl.BlockSpec(memory_space=pltpu.SMEM)
    step = jnp.where(row_id * 2 < row_size, 1, -1).reshape(1).astype(jnp.int32)
    send = pl.pallas_call(
        lambda *refs: send_kernel(*refs, ring=row_size),
        out_shape=jax.ShapeDtypeStruct((owners, width // PARTS, (PARTS - 1) * LANES), BF16),
        in_specs=[smem, vmem],
        out_specs=vmem,
        scratch_shapes=[pltpu.VMEM((owners * (width - width // PARTS), LANES), F32)],
        compiler_params=pltpu.CompilerParams(vmem_limit_bytes=4 * 2**20),
        name="pieces",
    )(step, features.transpose(0, 2, 1))
    recv = lax.all_to_all(send, ALL, split_axis=0, concat_axis=0, tiled=True)
    recv = recv.reshape(feat_size, row_size, width // PARTS, (PARTS - 1) * LANES)

    base = (feat_id * cycle + row_id * block_rows).reshape(1).astype(jnp.int32)
    ext = nodes + 2 * halo
    adj, ww = pl.pallas_call(
        lambda *refs: adjacency_kernel(*refs, cycle=cycle, slices=feat_size),
        out_shape=(
            jax.ShapeDtypeStruct((nodes, ext), BF16),
            jax.ShapeDtypeStruct((2 * n_features, hidden_width), BF16),
        ),
        in_specs=[smem, smem, smem, vmem, vmem],
        out_specs=(vmem, vmem),
        compiler_params=pltpu.CompilerParams(vmem_limit_bytes=2 * 2**20),
        cost_estimate=pl.CostEstimate(flops=2 * 10**6, bytes_accessed=4 * 10**6, transcendentals=0),
        name="adjacency",
    )(tile_cols, tile_counts, base, tiles, w_in)
    chips = feat_size // CORES
    half = jax.ShapeDtypeStruct((chips, width, hidden_width), F32)
    hidden, mine, other = pl.pallas_call(
        layer_kernel,
        out_shape=(jax.ShapeDtypeStruct((nodes, hidden_width), F32), half, half),
        in_specs=[vmem] * 5 + [smem],
        out_specs=(vmem, vmem, vmem),
        scratch_shapes=[pltpu.VMEM((ext, 2 * n_features), BF16)],
        compiler_params=pltpu.CompilerParams(vmem_limit_bytes=12 * 2**20),
        cost_estimate=pl.CostEstimate(flops=600 * 10**6, bytes_accessed=4 * 10**6, transcendentals=nodes * hidden_width),
        name="layer",
    )(recv, adj, ww, bias.reshape(1, hidden_width), cotangent, lax.axis_index("core").reshape(1))

    other = lax.ppermute(other, "core", [(0, 1), (1, 0)])
    hidden, other = lax.optimization_barrier((hidden.astype(BF16), other))
    pair = (mine + other).astype(BF16)
    copies = jnp.broadcast_to(pair[None], (row_size, chips, width, hidden_width))
    copies = copies.reshape(chips * row_size, width, hidden_width)
    pieces = lax.all_to_all(copies, ("rows", "x"), split_axis=0, concat_axis=0, tiled=True)
    return hidden, jnp.sum(pieces.astype(F32), axis=0)


def solution(mesh):
    devices = mesh.devices
    mesh = jax.sharding.Mesh(devices.reshape(devices.shape[0] // CORES, CORES, devices.shape[1]), ALL)
    in_specs = (
        P(FEAT, None, "rows"),
        P(),
        P(),
        P(ALL, None, None, None),
        P(ALL, None),
        P(ALL),
        P(ALL, None),
    )
    out_specs = (P(ALL, None), P(FEAT, None))
    return jax.shard_map(body, mesh=mesh, in_specs=in_specs, out_specs=out_specs, check_vma=False)
```
